32 devices in a mesh: groups: 2 (over y), person: 4 (over x, core), frame: 4 (over z).
Axes of the slice: x: 2, y: 2, z: 4, core: 2. Of those that a mesh axis runs over, the one named last changes fastest.
Arguments:
- tokens: bfloat16 [32, 256, 1024], P(('groups', 'person'), 'frame'), parts along dimension 0, may hold values from -6 to 6
- norm_time: float32 [1024], replicated, may hold values from 0.5 to 1.5
- qkv_time: bfloat16 [1024, 3072], replicated, may hold values from -0.1875 to 0.1875
- qgain_time: float32 [64], replicated, may hold values from 0.5 to 1.5
- kgain_time: float32 [64], replicated, may hold values from 0.5 to 1.5
- out_time: bfloat16 [1024, 1024], replicated, may hold values from -0.1875 to 0.1875
- norm_cross: float32 [1024], replicated, may hold values from 0.5 to 1.5
- qkv_cross: bfloat16 [1024, 3072], P('frame'), may hold values from -0.1875 to 0.1875
- qgain_cross: float32 [64], replicated, may hold values from 0.5 to 1.5
- kgain_cross: float32 [64], replicated, may hold values from 0.5 to 1.5
- out_cross: bfloat16 [1024, 1024], P('frame'), may hold values from -0.1875 to 0.1875
- frame_counts: int32 [32], P('groups'), parts along dimension 0, may hold values from 1 to 256, as said below
- presence: int32 [32], P('groups'), parts along dimension 0, may hold values 0 or 1
Outputs:
- block_out: bfloat16 [32, 256, 1024], P(('groups', 'person'), 'frame'), parts along dimension 0
The draws below stay inside these ranges and needn't reach their ends.
There are 2 independent parts, one for each index of `groups`. The reference program is written for one: setup_inputs(seed, part) draws one part's arguments, and reference() takes and returns one part's arrays. A program takes and returns all parts, laid end to end along the dimension named above; an argument that names none is the same for every part. Nothing has to cross between parts.
Inputs may be any that keep to these rules, and one draw needn't show every extreme that they name: `frame_counts`: some person has all 256 frames valid.
All inputs are finite; a program needn't handle non-finite values.
Results may differ from the reference program's by a relative error of at most 0.019.
Values may be sent and summed in bfloat16 or wider, within the bound.
A program may use at most 128 MiB of HBM per device.

```python
import math
import jax
import jax.numpy as jnp
from jax import lax

D = 1024
H = 16
HD = 64
P_SIZE = 16
F = 256


def draw_frame_counts(key, part):
    first_key, second_key = jax.random.split(jax.random.fold_in(key, 11))
    counts = jax.random.randint(first_key, (P_SIZE,), 1, F + 1, dtype=jnp.int32)
    chosen = jax.random.randint(second_key, (), 0, P_SIZE, dtype=jnp.int32)
    return jnp.where(jnp.arange(P_SIZE, dtype=jnp.int32) == chosen, F, counts).astype(jnp.int32)


def with_ends(drawn, stream_key, least, high):
    extent = drawn.shape
    place = [jax.random.randint(jax.random.fold_in(stream_key, axis), (), 0, extent[axis]) for axis in range(len(extent))]
    drawn = drawn.at[tuple(place)].set(least)
    longest = extent.index(max(extent))
    place[longest] = (place[longest] + 1) % extent[longest]
    return drawn.at[tuple(place)].set(high)


def block_scale(stream_key, extent, pieces, low, largest):
    gain, own = 1.0, jax.random.fold_in(stream_key, 6)
    for position, blocks in pieces:
        heights = jnp.exp(jax.random.uniform(jax.random.fold_in(own, position), (blocks,), jnp.float32, low / len(pieces), largest / len(pieces)))
        gain = gain * jnp.repeat(heights, extent[position] // blocks).reshape([-1 if axis == position else 1 for axis in range(len(extent))])
    return gain


def normal_values(own_key, shape, spread, most, cuts=(), held_as=jnp.bfloat16):
    values = spread * jax.random.normal(own_key, shape, jnp.float32)
    if cuts:
        values = values * block_scale(own_key, shape, cuts, -0.22, 0.18)
    return jnp.clip(values, -most, most).astype(held_as)


def setup_inputs(seed: int = 0, part: int = 0) -> dict:
    arg_keys = jax.random.split(jax.random.key(seed), 14)
    part_keys = jax.random.split(jax.random.fold_in(arg_keys[13], part), 14)
    return {
        "tokens": normal_values(part_keys[0], (P_SIZE, F, D), 1.0, 6.0, ((0, 4), (1, 4))),
        "norm_time": jnp.clip(1.0 + 0.1 * jax.random.normal(arg_keys[1], (D,), jnp.float32), 0.5, 1.5),
        "qkv_time": normal_values(arg_keys[2], (D, 3 * D), D ** -0.5, 0.1875),
        "qgain_time": jnp.clip(1.0 + 0.1 * jax.random.normal(arg_keys[3], (HD,), jnp.float32), 0.5, 1.5),
        "kgain_time": jnp.clip(1.0 + 0.1 * jax.random.normal(arg_keys[4], (HD,), jnp.float32), 0.5, 1.5),
        "out_time": normal_values(arg_keys[5], (D, D), D ** -0.5, 0.1875),
        "norm_cross": jnp.clip(1.0 + 0.1 * jax.random.normal(arg_keys[6], (D,), jnp.float32), 0.5, 1.5),
        "qkv_cross": normal_values(arg_keys[7], (D, 3 * D), D ** -0.5, 0.1875, ((0, 4),)),
        "qgain_cross": jnp.clip(1.0 + 0.1 * jax.random.normal(arg_keys[8], (HD,), jnp.float32), 0.5, 1.5),
        "kgain_cross": jnp.clip(1.0 + 0.1 * jax.random.normal(arg_keys[9], (HD,), jnp.float32), 0.5, 1.5),
        "out_cross": normal_values(arg_keys[10], (D, D), D ** -0.5, 0.1875, ((0, 4),)),
        "frame_counts": draw_frame_counts(jax.random.fold_in(jax.random.fold_in(arg_keys[13], part), 71), part),
        "presence": with_ends((jax.random.randint(part_keys[12], (P_SIZE,), 0, 4) < 3).astype(jnp.int32), jax.random.fold_in(part_keys[12], 1), 0, 1),
    }


def norm_rows(entries, gains):
    return entries * lax.rsqrt(lax.optimization_barrier(jnp.mean(entries * entries, axis=-1, keepdims=True)) + 1e-06) * gains

def project(hidden, weight, qgain, kgain):
    leading = hidden.shape[:-1]
    flat_rows = hidden.reshape(-1, hidden.shape[-1])
    joined = jnp.dot(flat_rows, weight, preferred_element_type=jnp.float32).reshape(leading + (3, H, HD))
    queries = (norm_rows(joined[..., 0, :, :], qgain) * (3.0 / math.sqrt(HD))).astype(jnp.bfloat16)
    key_rows = norm_rows(joined[..., 1, :, :], kgain).astype(jnp.bfloat16)
    value_rows = joined[..., 2, :, :].astype(jnp.bfloat16)
    return (queries, key_rows, value_rows)

def attend(queries, key_rows, value_rows, allowed):
    scores = jnp.einsum('qhd,khd->hqk', queries.astype(jnp.float32), key_rows.astype(jnp.float32))
    weights = jnp.where(allowed[None], jnp.exp(scores), 0.0).astype(jnp.bfloat16)
    totals = lax.optimization_barrier(jnp.sum(weights.astype(jnp.float32), axis=-1))
    summed = jnp.einsum('hqk,khd->qhd', weights.astype(jnp.float32), value_rows.astype(jnp.float32))
    return (summed / jnp.transpose(totals)[:, :, None]).astype(jnp.bfloat16)

def reference(tokens, norm_time, qkv_time, qgain_time, kgain_time, out_time, norm_cross, qkv_cross, qgain_cross, kgain_cross, out_cross, frame_counts, presence):
    stream = tokens.astype(jnp.float32)
    hidden = norm_rows(stream, norm_time).astype(jnp.bfloat16)
    queries, key_rows, value_rows = project(hidden, qkv_time, qgain_time, kgain_time)
    frames = jnp.arange(F, dtype=jnp.int32)
    live_frames = frames[None, :] < frame_counts[:, None]

    def person_step(member):
        query_one, key_one, value_one, live_one = member
        return attend(query_one, key_one, value_one, live_one[None, :])
    attended = lax.map(person_step, (queries, key_rows, value_rows, live_frames))
    branch = jnp.dot(attended.reshape(P_SIZE * F, D), out_time, preferred_element_type=jnp.float32).reshape(P_SIZE, F, D)
    middle = (stream + branch).astype(jnp.bfloat16)
    middle = lax.optimization_barrier(middle)
    stream = middle.astype(jnp.float32)
    hidden = norm_rows(stream, norm_cross).astype(jnp.bfloat16)
    queries, key_rows, value_rows = project(hidden, qkv_cross, qgain_cross, kgain_cross)
    present = (presence[:, None] == 1) & live_frames
    persons = jnp.arange(P_SIZE, dtype=jnp.int32)
    self_pair = persons[:, None] == persons[None, :]

    def frame_step(member):
        query_one, key_one, value_one, present_one = member
        return attend(query_one, key_one, value_one, present_one[None, :] | self_pair)
    order = (1, 0, 2, 3)
    attended = lax.map(frame_step, (jnp.transpose(queries, order), jnp.transpose(key_rows, order), jnp.transpose(value_rows, order), jnp.transpose(present)))
    attended = jnp.transpose(attended, order)
    branch = jnp.dot(attended.reshape(P_SIZE * F, D), out_cross, preferred_element_type=jnp.float32).reshape(P_SIZE, F, D)
    return (stream + branch).astype(jnp.bfloat16)
```

```python
import functools
import math

import jax
import jax.numpy as jnp
from jax import lax
from jax.experimental import pallas as pl
from jax.experimental.pallas import tpu as pltpu
from jax.sharding import PartitionSpec as P

H = 16
HD = 64
MESH = pl.DeviceIdType.MESH
F32 = jnp.float32
BF16 = jnp.bfloat16


def block_kernel(
    counts,
    present,
    tokens,
    norm_time,
    qkv_time,
    gain_time,
    out_time,
    norm_cross,
    qkv_cross,
    gain_cross,
    out_cross,
    out,
    tok,
    w_time,
    wo_time,
    w_cross,
    hid,
    att,
    bias,
    mid,
    mid_in,
    res,
    local_sem,
    tok_send,
    tok_recv,
    z_send,
    z_recv,
    hop_send,
    hop_recv,
    mid_send,
    mid_recv,
    out_send,
    out_recv,
):
    nz, nx = 4, 4
    group = lax.axis_index("groups")
    xc = lax.axis_index("person")
    z = lax.axis_index("frame")
    x, core = xc // 2, xc % 2
    rows, width = hid.shape
    frames = tok.shape[1]
    depth = qkv_cross.shape[0]
    piece = depth // 16
    part = frames // nx

    def zs(d):
        return (z - d + nz) % nz

    def zt(d):
        return (z + d) % nz

    def xs(i):
        return (xc - i + nx) % nx

    def xt(i):
        return (xc + i) % nx

    barrier = pltpu.get_barrier_semaphore()
    for i in range(nx):
        for d in range(nz):
            if i or d:
                pl.semaphore_signal(
                    barrier, inc=1, device_id={"person": xt(i), "frame": zt(d)}, device_id_type=MESH
                )
    pl.semaphore_signal(barrier, inc=1, device_id={"groups": 1 - group}, device_id_type=MESH)
    own = pl.multiple_of(z * depth, depth)
    local = [
        pltpu.make_async_copy(tokens.at[z], tok.at[z], local_sem.at[0]),
        pltpu.make_async_copy(qkv_time, w_time, local_sem.at[1]),
        pltpu.make_async_copy(out_time, wo_time, local_sem.at[2]),
        pltpu.make_async_copy(
            qkv_cross, w_cross.at[pl.ds(own, depth), pl.ds(0, 3 * width)], local_sem.at[3]
        ),
        pltpu.make_async_copy(
            out_cross, w_cross.at[pl.ds(own, depth), pl.ds(3 * width, width)], local_sem.at[4]
        ),
    ]
    for copy in local:
        copy.start()
    pl.semaphore_wait(barrier, nx * nz)

    def tok_copy(block, slot, d, peer):
        return pltpu.make_async_remote_copy(
            src_ref=tokens.at[block],
            dst_ref=tok.at[slot],
            send_sem=tok_send.at[d - 1],
            recv_sem=tok_recv.at[d - 1],
            device_id={"frame": peer},
            device_id_type=MESH,
        )

    for d in (2, 1, 3):
        tok_copy(zt(d), z, d, zt(d)).start()

    def at_piece(half):
        slot = core * 4 + (group * 2 + x if half == 0 else x * 2 + group)
        return half * (depth // 2) + slot * piece

    def z_copy(half, d, array, source, peer):
        start = pl.multiple_of(at_piece(half), piece)
        into = pl.multiple_of(source * depth + at_piece(half), piece)
        ref = (qkv_cross, out_cross)[array]
        columns = (pl.ds(0, 3 * width), pl.ds(3 * width, width))[array]
        return pltpu.make_async_remote_copy(
            src_ref=ref.at[pl.ds(start, piece), :],
            dst_ref=w_cross.at[pl.ds(into, piece), columns],
            send_sem=z_send.at[half, d - 1, array],
            recv_sem=z_recv.at[half, d - 1, array],
            device_id={"frame": peer},
            device_id_type=MESH,
        )

    for d in (1, 3, 2):
        for half in range(2):
            for array in range(2):
                z_copy(half, d, array, z, zt(d)).start()

    def hop_copy(hop, half, d, incoming):
        along_x = (half == 0) == (hop == 0)
        if hop == 2:
            side = 1 - core if incoming else core
            offset, length = side * 4, 4
            device = {"person": x * 2 + 1 - core}
        else:
            gx = (1 - x if incoming and along_x else x)
            gy = (1 - group if incoming and not along_x else group)
            if hop == 0:
                offset, length = core * 4 + (gy * 2 + gx if half == 0 else gx * 2 + gy), 1
            else:
                offset, length = core * 4 + (gy if half == 0 else gx) * 2, 2
            device = {"person": (1 - x) * 2 + core} if along_x else {"groups": 1 - group}
        start = pl.multiple_of(
            zs(d) * depth + half * (depth // 2) + offset * piece, length * piece
        )
        block = w_cross.at[pl.ds(start, length * piece), :]
        return pltpu.make_async_remote_copy(
            src_ref=block,
            dst_ref=block,
            send_sem=hop_send.at[hop, half, d - 1],
            recv_sem=hop_recv.at[hop, half, d - 1],
            device_id=device,
            device_id_type=MESH,
        )

    def forward(hop, d):
        for half in range(2):
            if hop == 0:
                for array in range(2):
                    z_copy(half, d, array, zs(d), zs(d)).wait_recv()
            else:
                hop_copy(hop - 1, half, d, True).wait_recv()
        for half in range(2):
            hop_copy(hop, half, d, False).start()

    lane = lax.broadcasted_iota(jnp.int32, (rows, 128), 1)
    low = lane < HD
    same_head = (
        lax.broadcasted_iota(jnp.int32, (256, 256), 0) // HD
        == lax.broadcasted_iota(jnp.int32, (256, 256), 1) // HD
    )
    blocks = jnp.where(same_head, 1.0, 0.0).astype(BF16)
    ones = jnp.ones((rows, 128), BF16)
    key_index = lax.broadcasted_iota(jnp.int32, (rows, rows), 1)
    query_index = lax.broadcasted_iota(jnp.int32, (rows, rows), 0)

    def normed(stream, gains):
        scale = lax.rsqrt(jnp.mean(stream * stream, axis=-1, keepdims=True) + 1e-06)
        return (stream * scale * gains).astype(BF16)

    def attend(weight, gain):
        hidden = hid[...]

        def project(column):
            return jnp.dot(hidden, weight[:, pl.ds(column, 256)], preferred_element_type=F32)

        def unit(entries):
            squares = jnp.dot((entries * entries).astype(BF16), blocks, preferred_element_type=F32)
            return entries * lax.rsqrt(squares * (1.0 / HD) + 1e-06)

        def step(t, carry):
            column = pl.multiple_of(t * 256, 256)
            queries = unit(project(column)) * gain[...]
            keys = unit(project(width + column)).astype(BF16)
            values = project(2 * width + column).astype(BF16)
            for pair in range(2):
                lanes = slice(pair * 128, (pair + 1) * 128)
                two = queries[:, lanes]
                extended = jnp.concatenate([values[:, lanes], ones], axis=1)
                sums = []
                for member in range(2):
                    one = jnp.where(low if member == 0 else ~low, two, 0.0).astype(BF16)
                    scores = lax.dot_general(
                        one, keys[:, lanes], (((1,), (1,)), ((), ())), preferred_element_type=F32
                    )
                    weights = jnp.exp(scores + bias[...]).astype(BF16)
                    sums.append(jnp.dot(weights, extended, preferred_element_type=F32))
                summed = jnp.where(low, sums[0][:, :128], sums[1][:, :128])
                total = jnp.where(low, sums[0][:, 128:], sums[1][:, 128:])
                att[:, pl.ds(column + pair * 128, 128)] = (summed / total).astype(BF16)
            return carry

        lax.fori_loop(0, width // 256, step, 0)

    person = xc * nz + z
    bias[...] = jnp.where(key_index < counts[person], 0.0, -1e30)
    local[0].wait()
    for d in (1, 3, 2):
        tok_copy(zs(d), zs(d), d, zs(d)).wait_recv()
    hid[...] = normed(tok[...].reshape(rows, width).astype(F32), norm_time[...])
    local[1].wait()
    attend(w_time, gain_time)
    local[2].wait()

    def temporal_out(t, carry):
        column = pl.multiple_of(t * 256, 256)
        branch = jnp.dot(att[...], wo_time[:, pl.ds(column, 256)], preferred_element_type=F32)
        stream = tok[:, :, pl.ds(column, 256)].reshape(rows, 256).astype(F32)
        mid[:, pl.ds(column, 256)] = (stream + branch).astype(BF16)
        return carry

    lax.fori_loop(0, width // 256, temporal_out, 0)

    def mid_copy(i, d, take_x, take_z, owner, peer):
        start = pl.multiple_of(take_z * frames + take_x * part, part)
        into = pl.multiple_of(owner * part, part)
        return pltpu.make_async_remote_copy(
            src_ref=mid.at[pl.ds(start, part), :],
            dst_ref=mid_in.at[pl.ds(into, part), :],
            send_sem=mid_send.at[i, d],
            recv_sem=mid_recv.at[i, d],
            device_id=peer,
            device_id_type=MESH,
        )

    offsets = [(i, d) for d in (2, 1, 3, 0) for i in range(nx) if i or d]
    for i, d in offsets:
        mid_copy(i, d, xt(i), zt(d), person, {"person": xt(i), "frame": zt(d)}).start()
    into = pl.multiple_of(person * part, part)
    start = pl.multiple_of(z * frames + xc * part, part)
    mid_in[pl.ds(into, part), :] = mid[pl.ds(start, part), :]

    for d in (1, 3, 2):
        forward(0, d)

    key_row = lax.broadcasted_iota(jnp.int32, (8, rows), 1)
    limit = jnp.zeros((8, rows), jnp.int32)
    for member in range(nx * nz):
        valid = jnp.where(present[member] == 1, counts[member], 0)
        limit = jnp.where(key_row // part == member, valid, limit)
    frame = z * frames + xc * part + key_row % part
    usable = jnp.broadcast_to(jnp.where(frame < limit, 1, 0)[:1, :], (rows, rows))
    allowed = ((key_index % part == query_index % part) & (usable > 0)) | (key_index == query_index)
    bias[...] = jnp.where(allowed, 0.0, -1e30)

    for d in (1, 3, 2):
        forward(1, d)
    for i, d in offsets:
        source = xs(i) * nz + zs(d)
        mid_copy(i, d, xc, z, source, {"person": xs(i), "frame": zs(d)}).wait_recv()
    hid[...] = normed(mid_in[...].astype(F32), norm_cross[...])
    for d in (1, 3, 2):
        forward(2, d)
    local[3].wait()
    local[4].wait()
    for d in (1, 3, 2):
        for half in range(2):
            hop_copy(2, half, d, True).wait_recv()
    attend(w_cross, gain_cross)

    def cross_out(t, carry):
        column = pl.multiple_of(t * 256, 256)
        branch = jnp.dot(
            att[...], w_cross[:, pl.ds(3 * width + column, 256)], preferred_element_type=F32
        )
        total = mid_in[:, pl.ds(column, 256)].astype(F32) + branch
        res[:, :, pl.ds(column, 256)] = total.astype(BF16).reshape(nx * nz, part, 256)
        return carry

    lax.fori_loop(0, width // 256, cross_out, 0)

    def out_copy(i, block, slot, peer):
        return pltpu.make_async_remote_copy(
            src_ref=res.at[pl.ds(block * nz, nz)],
            dst_ref=out.at[:, pl.ds(pl.multiple_of(slot * part, part), part), :],
            send_sem=out_send.at[i - 1],
            recv_sem=out_recv.at[i - 1],
            device_id={"person": peer},
            device_id_type=MESH,
        )

    for i in (2, 3, 1):
        out_copy(i, xt(i), xc, xt(i)).start()
    kept = pltpu.make_async_copy(
        res.at[pl.ds(xc * nz, nz)],
        out.at[:, pl.ds(pl.multiple_of(xc * part, part), part), :],
        local_sem.at[5],
    )
    kept.start()
    for d in (1, 2, 3):
        tok_copy(zt(d), z, d, zt(d)).wait_send()
        for half in range(2):
            for array in range(2):
                z_copy(half, d, array, z, zt(d)).wait_send()
            for hop in range(3):
                hop_copy(hop, half, d, False).wait_send()
    for i, d in offsets:
        mid_copy(i, d, xt(i), zt(d), person, {"person": xt(i), "frame": zt(d)}).wait_send()
    kept.wait()
    for i in (1, 2, 3):
        out_copy(i, xt(i), xc, xt(i)).wait_send()
        out_copy(i, xs(i), xs(i), xs(i)).wait_recv()


def whole_block(
    tokens,
    norm_time,
    qkv_time,
    qgain_time,
    kgain_time,
    out_time,
    norm_cross,
    qkv_cross,
    qgain_cross,
    kgain_cross,
    out_cross,
    frame_counts,
    presence,
):
    persons, frames, width = tokens.shape
    rows = persons * frames
    scale = 3.0 / math.sqrt(HD)
    gain_time = jnp.tile(qgain_time * kgain_time * scale, 4)[None, :]
    gain_cross = jnp.tile(qgain_cross * kgain_cross * scale, 4)[None, :]
    smem = pl.BlockSpec(memory_space=pltpu.SMEM)
    vmem = pl.BlockSpec(memory_space=pltpu.VMEM)
    anywhere = pl.BlockSpec(memory_space=pl.ANY)
    dma = pltpu.SemaphoreType.DMA
    return pl.pallas_call(
        block_kernel,
        out_shape=jax.ShapeDtypeStruct(tokens.shape, BF16),
        in_specs=[
            smem,
            smem,
            anywhere,
            vmem,
            anywhere,
            vmem,
            anywhere,
            vmem,
            anywhere,
            vmem,
            anywhere,
        ],
        out_specs=anywhere,
        scratch_shapes=[
            pltpu.VMEM(tokens.shape, BF16),
            pltpu.VMEM((width, 3 * width), BF16),
            pltpu.VMEM((width, width), BF16),
            pltpu.VMEM((width, 4 * width), BF16),
            pltpu.VMEM((rows, width), BF16),
            pltpu.VMEM((rows, width), BF16),
            pltpu.VMEM((rows, rows), F32),
            pltpu.VMEM((rows, width), BF16),
            pltpu.VMEM((rows, width), BF16),
            pltpu.VMEM((16, rows // 16, width), BF16),
            dma((6,)),
            dma((3,)),
            dma((3,)),
            dma((2, 3, 2)),
            dma((2, 3, 2)),
            dma((3, 2, 3)),
            dma((3, 2, 3)),
            dma((4, 4)),
            dma((4, 4)),
            dma((3,)),
            dma((3,)),
        ],
        compiler_params=pltpu.CompilerParams(
            collective_id=0, has_side_effects=True, vmem_limit_bytes=48 * 1024 * 1024
        ),
    )(
        frame_counts,
        presence,
        tokens,
        norm_time[None, :],
        qkv_time,
        gain_time,
        out_time,
        norm_cross[None, :],
        qkv_cross,
        gain_cross,
        out_cross,
    )


def norm_rows(entries, gains):
    return entries * lax.rsqrt(jnp.mean(entries * entries, axis=-1, keepdims=True) + 1e-06) * gains


def project(hidden, weight, qgain, kgain):
    leading = hidden.shape[:-1]
    flat_rows = hidden.reshape(-1, hidden.shape[-1])
    joined = jnp.dot(flat_rows, weight, preferred_element_type=jnp.float32).reshape(
        leading + (3, H, HD)
    )
    queries = (norm_rows(joined[..., 0, :, :], qgain) * (3.0 / math.sqrt(HD))).astype(jnp.bfloat16)
    key_rows = norm_rows(joined[..., 1, :, :], kgain).astype(jnp.bfloat16)
    value_rows = joined[..., 2, :, :].astype(jnp.bfloat16)
    return (queries, key_rows, value_rows)


def on_device(
    tokens,
    norm_time,
    qkv_time,
    qgain_time,
    kgain_time,
    out_time,
    norm_cross,
    qkv_cross,
    qgain_cross,
    kgain_cross,
    out_cross,
    frame_counts,
    presence,
):
    person_rows, frame_rows, width = tokens.shape
    person_base = lax.axis_index("person") * person_rows
    frame_base = lax.axis_index("frame") * frame_rows
    cross_qkv, cross_out = (
        lax.all_gather(qkv_cross, "frame", axis=0, tiled=True),
        lax.all_gather(out_cross, "frame", axis=0, tiled=True),
    )
    local_counts = lax.dynamic_slice_in_dim(frame_counts, person_base, person_rows)
    local_present = lax.dynamic_slice_in_dim(presence, person_base, person_rows)
    frame_index = frame_base + jnp.arange(frame_rows, dtype=jnp.int32)
    live_frames = frame_index[None, :] < local_counts[:, None]
    key_flags_time = live_frames.astype(jnp.int32)
    key_flags_cross = (live_frames & (local_present[:, None] == 1)).astype(jnp.int32)
    stream = tokens.astype(jnp.float32)
    hidden = norm_rows(stream, norm_time).astype(jnp.bfloat16)
    queries, key_rows, value_rows = project(hidden, qkv_time, qgain_time, kgain_time)
    spread_flags = jnp.broadcast_to(
        key_flags_time[:, :, None, None], (person_rows, frame_rows, H, 1)
    )

    def attend_one(member):
        query_one, key_one, value_one, flag_one = member
        scores = jnp.einsum("qhd,khd->hqk", query_one, key_one, preferred_element_type=jnp.float32)
        allowed = (flag_one[:, 0, 0] > 0)[None, None, :]
        weights = jnp.where(allowed, jnp.exp(scores), 0.0).astype(jnp.bfloat16)
        summed = jnp.einsum("hqk,khd->qhd", weights, value_one, preferred_element_type=jnp.float32)
        totals = jnp.transpose(jnp.sum(weights.astype(jnp.float32), axis=-1))
        return (summed / totals[:, :, None]).astype(jnp.bfloat16)

    results = lax.map(
        attend_one,
        (
            lax.all_to_all(queries, "frame", split_axis=2, concat_axis=1, tiled=True),
            lax.all_to_all(key_rows, "frame", split_axis=2, concat_axis=1, tiled=True),
            lax.all_to_all(value_rows, "frame", split_axis=2, concat_axis=1, tiled=True),
            lax.all_to_all(spread_flags, "frame", split_axis=2, concat_axis=1, tiled=True),
        ),
    )
    attended = lax.all_to_all(results, "frame", split_axis=1, concat_axis=2, tiled=True)
    token_count = person_rows * frame_rows
    branch = jnp.dot(
        attended.reshape(token_count, width), out_time, preferred_element_type=jnp.float32
    ).reshape(person_rows, frame_rows, width)
    middle = (stream + branch).astype(jnp.bfloat16)
    middle = lax.optimization_barrier(middle)
    stream = middle.astype(jnp.float32)
    hidden = norm_rows(stream, norm_cross).astype(jnp.bfloat16)
    queries, key_rows, value_rows = project(hidden, cross_qkv, qgain_cross, kgain_cross)
    spread_flags = jnp.broadcast_to(
        key_flags_cross[:, :, None, None], (person_rows, frame_rows, H, 1)
    )
    query_all = lax.all_to_all(queries, "person", split_axis=2, concat_axis=0, tiled=True)
    key_all = lax.all_to_all(key_rows, "person", split_axis=2, concat_axis=0, tiled=True)
    value_all = lax.all_to_all(value_rows, "person", split_axis=2, concat_axis=0, tiled=True)
    flag_all = lax.all_to_all(spread_flags, "person", split_axis=2, concat_axis=0, tiled=True)
    people = query_all.shape[0]
    scores = jnp.einsum("qfhd,kfhd->fhqk", query_all, key_all, preferred_element_type=jnp.float32)
    persons = jnp.arange(people, dtype=jnp.int32)
    self_pair = persons[:, None] == persons[None, :]
    allowed = (jnp.transpose(flag_all[:, :, 0, 0])[:, None, None, :] > 0) | self_pair[None, None]
    weights = jnp.where(allowed, jnp.exp(scores), 0.0).astype(jnp.bfloat16)
    summed = jnp.einsum("fhqk,kfhd->qfhd", weights, value_all, preferred_element_type=jnp.float32)
    totals = jnp.transpose(jnp.sum(weights.astype(jnp.float32), axis=3), (2, 0, 1))
    results = (summed / totals[..., None]).astype(jnp.bfloat16)
    attended = lax.all_to_all(results, "person", split_axis=0, concat_axis=2, tiled=True)
    branch = jnp.dot(
        attended.reshape(token_count, width), cross_out, preferred_element_type=jnp.float32
    ).reshape(person_rows, frame_rows, width)
    return (stream + branch).astype(jnp.bfloat16)


def solution(mesh):
    placed = (
        P(("groups", "person"), "frame", None),
        P(),
        P(),
        P(),
        P(),
        P(),
        P(),
        P("frame", None),
        P(),
        P(),
        P("frame", None),
        P("groups"),
        P("groups"),
    )
    sizes = dict(mesh.shape)
    fits = sizes == {"groups": 2, "person": 4, "frame": 4}
    return jax.shard_map(
        whole_block if fits else on_device,
        mesh=mesh,
        in_specs=placed,
        out_specs=P(("groups", "person"), "frame", None),
        check_vma=False,
    )
```

```python
import functools
import math

import jax
import jax.numpy as jnp
from jax import lax
from jax.experimental import pallas as pl
from jax.experimental.pallas import tpu as pltpu
from jax.sharding import PartitionSpec as P

H = 16
HD = 64
MESH = pl.DeviceIdType.MESH
F32 = jnp.float32
BF16 = jnp.bfloat16


def block_kernel(
    tokens,
    qkv_time,
    out_time,
    qkv_cross,
    out_cross,
    counts_in,
    present_in,
    norm_time_in,
    norm_cross_in,
    qgain_time_in,
    kgain_time_in,
    qgain_cross_in,
    kgain_cross_in,
    out,
    counts,
    present,
    norm_time,
    norm_cross,
    qgain_time,
    kgain_time,
    qgain_cross,
    kgain_cross,
    tok,
    w_time,
    wo_time,
    w_cross,
    hid,
    att,
    bias,
    mid,
    mid_in,
    res,
    local_sem,
    small_sem,
    tok_send,
    tok_recv,
    z_send,
    z_recv,
    hop_send,
    hop_recv,
    mid_send,
    mid_recv,
    out_send,
    out_recv,
):
    nz, nx = 4, 4
    group = lax.axis_index("groups")
    xc = lax.axis_index("person")
    z = lax.axis_index("frame")
    x, core = xc // 2, xc % 2
    rows, width = hid.shape
    frames = tok.shape[1]
    depth = qkv_cross.shape[0]
    piece = depth // 16
    part = frames // nx

    def zs(d):
        return (z - d + nz) % nz

    def zt(d):
        return (z + d) % nz

    def xs(i):
        return (xc - i + nx) % nx

    def xt(i):
        return (xc + i) % nx

    barrier = pltpu.get_barrier_semaphore()
    for i in range(nx):
        for d in range(nz):
            if i or d:
                pl.semaphore_signal(
                    barrier, inc=1, device_id={"person": xt(i), "frame": zt(d)}, device_id_type=MESH
                )
    pl.semaphore_signal(barrier, inc=1, device_id={"groups": 1 - group}, device_id_type=MESH)
    own = pl.multiple_of(z * depth, depth)
    local = [
        pltpu.make_async_copy(tokens.at[z], tok.at[z], local_sem.at[0]),
        pltpu.make_async_copy(qkv_time, w_time, local_sem.at[1]),
        pltpu.make_async_copy(out_time, wo_time, local_sem.at[2]),
        pltpu.make_async_copy(
            qkv_cross, w_cross.at[pl.ds(own, depth), pl.ds(0, 3 * width)], local_sem.at[3]
        ),
        pltpu.make_async_copy(
            out_cross, w_cross.at[pl.ds(own, depth), pl.ds(3 * width, width)], local_sem.at[4]
        ),
    ]
    small = [
        pltpu.make_async_copy(source, target, small_sem.at[k])
        for k, (source, target) in enumerate(
            (
                (counts_in, counts),
                (present_in, present),
                (norm_time_in, norm_time),
                (norm_cross_in, norm_cross),
                (qgain_time_in, qgain_time),
                (kgain_time_in, kgain_time),
                (qgain_cross_in, qgain_cross),
                (kgain_cross_in, kgain_cross),
            )
        )
    ]
    for copy in small + local:
        copy.start()
    pl.semaphore_wait(barrier, nx * nz)

    def tok_copy(block, slot, d, peer):
        return pltpu.make_async_remote_copy(
            src_ref=tokens.at[block],
            dst_ref=tok.at[slot],
            send_sem=tok_send.at[d - 1],
            recv_sem=tok_recv.at[d - 1],
            device_id={"frame": peer},
            device_id_type=MESH,
        )

    for d in (2, 1, 3):
        tok_copy(zt(d), z, d, zt(d)).start()

    def at_piece(half):
        slot = core * 4 + (group * 2 + x if half == 0 else x * 2 + group)
        return half * (depth // 2) + slot * piece

    def z_copy(half, d, array, source, peer):
        start = pl.multiple_of(at_piece(half), piece)
        into = pl.multiple_of(source * depth + at_piece(half), piece)
        ref = (qkv_cross, out_cross)[array]
        columns = (pl.ds(0, 3 * width), pl.ds(3 * width, width))[array]
        return pltpu.make_async_remote_copy(
            src_ref=ref.at[pl.ds(start, piece), :],
            dst_ref=w_cross.at[pl.ds(into, piece), columns],
            send_sem=z_send.at[half, d - 1, array],
            recv_sem=z_recv.at[half, d - 1, array],
            device_id={"frame": peer},
            device_id_type=MESH,
        )

    for d in (1, 3, 2):
        for half in range(2):
            for array in range(2):
                z_copy(half, d, array, z, zt(d)).start()

    def hop_copy(hop, half, d, incoming):
        along_x = (half == 0) == (hop == 0)
        if hop == 2:
            side = 1 - core if incoming else core
            offset, length = side * 4, 4
            device = {"person": x * 2 + 1 - core}
        else:
            gx = (1 - x if incoming and along_x else x)
            gy = (1 - group if incoming and not along_x else group)
            if hop == 0:
                offset, length = core * 4 + (gy * 2 + gx if half == 0 else gx * 2 + gy), 1
            else:
                offset, length = core * 4 + (gy if half == 0 else gx) * 2, 2
            device = {"person": (1 - x) * 2 + core} if along_x else {"groups": 1 - group}
        start = pl.multiple_of(
            zs(d) * depth + half * (depth // 2) + offset * piece, length * piece
        )
        block = w_cross.at[pl.ds(start, length * piece), :]
        return pltpu.make_async_remote_copy(
            src_ref=block,
            dst_ref=block,
            send_sem=hop_send.at[hop, half, d - 1],
            recv_sem=hop_recv.at[hop, half, d - 1],
            device_id=device,
            device_id_type=MESH,
        )

    def forward(hop, d):
        for half in range(2):
            if hop == 0:
                for array in range(2):
                    z_copy(half, d, array, zs(d), zs(d)).wait_recv()
            else:
                hop_copy(hop - 1, half, d, True).wait_recv()
        for half in range(2):
            hop_copy(hop, half, d, False).start()

    lane = lax.broadcasted_iota(jnp.int32, (rows, 128), 1)
    low = lane < HD
    same_head = (
        lax.broadcasted_iota(jnp.int32, (256, 256), 0) // HD
        == lax.broadcasted_iota(jnp.int32, (256, 256), 1) // HD
    )
    blocks = jnp.where(same_head, 1.0, 0.0).astype(BF16)
    ones = jnp.ones((rows, 128), BF16)
    key_index = lax.broadcasted_iota(jnp.int32, (rows, rows), 1)
    query_index = lax.broadcasted_iota(jnp.int32, (rows, rows), 0)

    def normed(stream, gains):
        scale = lax.rsqrt(jnp.mean(stream * stream, axis=-1, keepdims=True) + 1e-06)
        return (stream * scale * gains).astype(BF16)

    def attend(weight, qgain, kgain, after):
        hidden = hid[...]
        once = qgain[...] * kgain[...] * (3.0 / math.sqrt(HD))
        gain = jnp.concatenate([once] * 4, axis=1)

        def project(column):
            return jnp.dot(hidden, weight[:, pl.ds(column, 256)], preferred_element_type=F32)

        def unit(entries):
            squares = jnp.dot((entries * entries).astype(BF16), blocks, preferred_element_type=F32)
            return entries * lax.rsqrt(squares * (1.0 / HD) + 1e-06)

        for t in range(width // 256):
            column = t * 256
            queries = unit(project(column)) * gain
            keys = unit(project(width + column)).astype(BF16)
            values = project(2 * width + column).astype(BF16)
            for pair in range(2):
                lanes = slice(pair * 128, (pair + 1) * 128)
                two = queries[:, lanes]
                extended = jnp.concatenate([values[:, lanes], ones], axis=1)
                sums = []
                for member in range(2):
                    one = jnp.where(low if member == 0 else ~low, two, 0.0).astype(BF16)
                    scores = lax.dot_general(
                        one, keys[:, lanes], (((1,), (1,)), ((), ())), preferred_element_type=F32
                    )
                    weights = jnp.exp(scores + bias[...]).astype(BF16)
                    sums.append(jnp.dot(weights, extended, preferred_element_type=F32))
                summed = jnp.where(low, sums[0][:, :128], sums[1][:, :128])
                total = jnp.where(low, sums[0][:, 128:], sums[1][:, 128:])
                att[:, pl.ds(column + pair * 128, 128)] = (summed / total).astype(BF16)
            after(t)

    person = xc * nz + z
    for copy in small:
        copy.wait()
    bias[...] = jnp.where(key_index < counts[person], 0.0, -1e30)
    local[0].wait()
    for d in (1, 3, 2):
        tok_copy(zs(d), zs(d), d, zs(d)).wait_recv()
    hid[...] = normed(tok[...].reshape(rows, width).astype(F32), norm_time[...])
    local[1].wait()
    early = {0: 1, 1: 3, 2: 2}

    def spread(t):
        if t in early:
            forward(0, early[t])

    attend(w_time, qgain_time, kgain_time, spread)
    local[2].wait()

    def temporal_out(t, carry):
        column = pl.multiple_of(t * 256, 256)
        branch = jnp.dot(att[...], wo_time[:, pl.ds(column, 256)], preferred_element_type=F32)
        stream = tok[:, :, pl.ds(column, 256)].reshape(rows, 256).astype(F32)
        mid[:, pl.ds(column, 256)] = (stream + branch).astype(BF16)
        return carry

    lax.fori_loop(0, width // 256, temporal_out, 0)

    def mid_copy(i, d, take_x, take_z, owner, peer):
        start = pl.multiple_of(take_z * frames + take_x * part, part)
        into = pl.multiple_of(owner * part, part)
        return pltpu.make_async_remote_copy(
            src_ref=mid.at[pl.ds(start, part), :],
            dst_ref=mid_in.at[pl.ds(into, part), :],
            send_sem=mid_send.at[i, d],
            recv_sem=mid_recv.at[i, d],
            device_id=peer,
            device_id_type=MESH,
        )

    offsets = [(i, d) for d in (2, 1, 3, 0) for i in range(nx) if i or d]
    for i, d in offsets:
        mid_copy(i, d, xt(i), zt(d), person, {"person": xt(i), "frame": zt(d)}).start()
    into = pl.multiple_of(person * part, part)
    start = pl.multiple_of(z * frames + xc * part, part)
    mid_in[pl.ds(into, part), :] = mid[pl.ds(start, part), :]

    for d in (1, 3, 2):
        forward(1, d)

    key_row = lax.broadcasted_iota(jnp.int32, (8, rows), 1)
    limit = jnp.zeros((8, rows), jnp.int32)
    for member in range(nx * nz):
        valid = jnp.where(present[member] == 1, counts[member], 0)
        limit = jnp.where(key_row // part == member, valid, limit)
    frame = z * frames + xc * part + key_row % part
    usable = jnp.broadcast_to(jnp.where(frame < limit, 1, 0)[:1, :], (rows, rows))
    allowed = ((key_index % part == query_index % part) & (usable > 0)) | (key_index == query_index)
    bias[...] = jnp.where(allowed, 0.0, -1e30)

    for d in (1, 3, 2):
        forward(2, d)
    for i, d in offsets:
        source = xs(i) * nz + zs(d)
        mid_copy(i, d, xc, z, source, {"person": xs(i), "frame": zs(d)}).wait_recv()
    hid[...] = normed(mid_in[...].astype(F32), norm_cross[...])
    local[3].wait()
    local[4].wait()
    for d in (1, 3, 2):
        for half in range(2):
            hop_copy(2, half, d, True).wait_recv()
    attend(w_cross, qgain_cross, kgain_cross, lambda t: None)

    def cross_out(t, carry):
        column = pl.multiple_of(t * 256, 256)
        branch = jnp.dot(
            att[...], w_cross[:, pl.ds(3 * width + column, 256)], preferred_element_type=F32
        )
        total = mid_in[:, pl.ds(column, 256)].astype(F32) + branch
        res[:, :, pl.ds(column, 256)] = total.astype(BF16).reshape(nx * nz, part, 256)
        return carry

    lax.fori_loop(0, width // 256, cross_out, 0)

    def out_copy(i, block, slot, peer):
        return pltpu.make_async_remote_copy(
            src_ref=res.at[pl.ds(block * nz, nz)],
            dst_ref=out.at[:, pl.ds(pl.multiple_of(slot * part, part), part), :],
            send_sem=out_send.at[i - 1],
            recv_sem=out_recv.at[i - 1],
            device_id={"person": peer},
            device_id_type=MESH,
        )

    for i in (2, 3, 1):
        out_copy(i, xt(i), xc, xt(i)).start()
    kept = pltpu.make_async_copy(
        res.at[pl.ds(xc * nz, nz)],
        out.at[:, pl.ds(pl.multiple_of(xc * part, part), part), :],
        local_sem.at[5],
    )
    kept.start()
    for d in (1, 2, 3):
        tok_copy(zt(d), z, d, zt(d)).wait_send()
        for half in range(2):
            for array in range(2):
                z_copy(half, d, array, z, zt(d)).wait_send()
            for hop in range(3):
                hop_copy(hop, half, d, False).wait_send()
    for i, d in offsets:
        mid_copy(i, d, xt(i), zt(d), person, {"person": xt(i), "frame": zt(d)}).wait_send()
    kept.wait()
    for i in (1, 2, 3):
        out_copy(i, xt(i), xc, xt(i)).wait_send()
        out_copy(i, xs(i), xs(i), xs(i)).wait_recv()


def whole_block(
    tokens,
    norm_time,
    qkv_time,
    qgain_time,
    kgain_time,
    out_time,
    norm_cross,
    qkv_cross,
    qgain_cross,
    kgain_cross,
    out_cross,
    frame_counts,
    presence,
):
    persons, frames, width = tokens.shape
    rows = persons * frames
    anywhere = pl.BlockSpec(memory_space=pl.ANY)
    dma = pltpu.SemaphoreType.DMA
    return pl.pallas_call(
        block_kernel,
        out_shape=jax.ShapeDtypeStruct(tokens.shape, BF16),
        in_specs=[anywhere] * 13,
        out_specs=anywhere,
        scratch_shapes=[
            pltpu.SMEM(frame_counts.shape, jnp.int32),
            pltpu.SMEM(presence.shape, jnp.int32),
            pltpu.VMEM((1, width), F32),
            pltpu.VMEM((1, width), F32),
            pltpu.VMEM((1, HD), F32),
            pltpu.VMEM((1, HD), F32),
            pltpu.VMEM((1, HD), F32),
            pltpu.VMEM((1, HD), F32),
            pltpu.VMEM(tokens.shape, BF16),
            pltpu.VMEM((width, 3 * width), BF16),
            pltpu.VMEM((width, width), BF16),
            pltpu.VMEM((width, 4 * width), BF16),
            pltpu.VMEM((rows, width), BF16),
            pltpu.VMEM((rows, width), BF16),
            pltpu.VMEM((rows, rows), F32),
            pltpu.VMEM((rows, width), BF16),
            pltpu.VMEM((rows, width), BF16),
            pltpu.VMEM((16, rows // 16, width), BF16),
            dma((6,)),
            dma((8,)),
            dma((3,)),
            dma((3,)),
            dma((2, 3, 2)),
            dma((2, 3, 2)),
            dma((3, 2, 3)),
            dma((3, 2, 3)),
            dma((4, 4)),
            dma((4, 4)),
            dma((3,)),
            dma((3,)),
        ],
        compiler_params=pltpu.CompilerParams(
            collective_id=0, has_side_effects=True, vmem_limit_bytes=60 * 1024 * 1024
        ),
    )(
        tokens,
        qkv_time,
        out_time,
        qkv_cross,
        out_cross,
        frame_counts,
        presence,
        norm_time[None, :],
        norm_cross[None, :],
        qgain_time[None, :],
        kgain_time[None, :],
        qgain_cross[None, :],
        kgain_cross[None, :],
    )


def norm_rows(entries, gains):
    return entries * lax.rsqrt(jnp.mean(entries * entries, axis=-1, keepdims=True) + 1e-06) * gains


def project(hidden, weight, qgain, kgain):
    leading = hidden.shape[:-1]
    flat_rows = hidden.reshape(-1, hidden.shape[-1])
    joined = jnp.dot(flat_rows, weight, preferred_element_type=jnp.float32).reshape(
        leading + (3, H, HD)
    )
    queries = (norm_rows(joined[..., 0, :, :], qgain) * (3.0 / math.sqrt(HD))).astype(jnp.bfloat16)
    key_rows = norm_rows(joined[..., 1, :, :], kgain).astype(jnp.bfloat16)
    value_rows = joined[..., 2, :, :].astype(jnp.bfloat16)
    return (queries, key_rows, value_rows)


def on_device(
    tokens,
    norm_time,
    qkv_time,
    qgain_time,
    kgain_time,
    out_time,
    norm_cross,
    qkv_cross,
    qgain_cross,
    kgain_cross,
    out_cross,
    frame_counts,
    presence,
):
    person_rows, frame_rows, width = tokens.shape
    person_base = lax.axis_index("person") * person_rows
    frame_base = lax.axis_index("frame") * frame_rows
    cross_qkv, cross_out = (
        lax.all_gather(qkv_cross, "frame", axis=0, tiled=True),
        lax.all_gather(out_cross, "frame", axis=0, tiled=True),
    )
    local_counts = lax.dynamic_slice_in_dim(frame_counts, person_base, person_rows)
    local_present = lax.dynamic_slice_in_dim(presence, person_base, person_rows)
    frame_index = frame_base + jnp.arange(frame_rows, dtype=jnp.int32)
    live_frames = frame_index[None, :] < local_counts[:, None]
    key_flags_time = live_frames.astype(jnp.int32)
    key_flags_cross = (live_frames & (local_present[:, None] == 1)).astype(jnp.int32)
    stream = tokens.astype(jnp.float32)
    hidden = norm_rows(stream, norm_time).astype(jnp.bfloat16)
    queries, key_rows, value_rows = project(hidden, qkv_time, qgain_time, kgain_time)
    spread_flags = jnp.broadcast_to(
        key_flags_time[:, :, None, None], (person_rows, frame_rows, H, 1)
    )

    def attend_one(member):
        query_one, key_one, value_one, flag_one = member
        scores = jnp.einsum("qhd,khd->hqk", query_one, key_one, preferred_element_type=jnp.float32)
        allowed = (flag_one[:, 0, 0] > 0)[None, None, :]
        weights = jnp.where(allowed, jnp.exp(scores), 0.0).astype(jnp.bfloat16)
        summed = jnp.einsum("hqk,khd->qhd", weights, value_one, preferred_element_type=jnp.float32)
        totals = jnp.transpose(jnp.sum(weights.astype(jnp.float32), axis=-1))
        return (summed / totals[:, :, None]).astype(jnp.bfloat16)

    results = lax.map(
        attend_one,
        (
            lax.all_to_all(queries, "frame", split_axis=2, concat_axis=1, tiled=True),
            lax.all_to_all(key_rows, "frame", split_axis=2, concat_axis=1, tiled=True),
            lax.all_to_all(value_rows, "frame", split_axis=2, concat_axis=1, tiled=True),
            lax.all_to_all(spread_flags, "frame", split_axis=2, concat_axis=1, tiled=True),
        ),
    )
    attended = lax.all_to_all(results, "frame", split_axis=1, concat_axis=2, tiled=True)
    token_count = person_rows * frame_rows
    branch = jnp.dot(
        attended.reshape(token_count, width), out_time, preferred_element_type=jnp.float32
    ).reshape(person_rows, frame_rows, width)
    middle = (stream + branch).astype(jnp.bfloat16)
    middle = lax.optimization_barrier(middle)
    stream = middle.astype(jnp.float32)
    hidden = norm_rows(stream, norm_cross).astype(jnp.bfloat16)
    queries, key_rows, value_rows = project(hidden, cross_qkv, qgain_cross, kgain_cross)
    spread_flags = jnp.broadcast_to(
        key_flags_cross[:, :, None, None], (person_rows, frame_rows, H, 1)
    )
    query_all = lax.all_to_all(queries, "person", split_axis=2, concat_axis=0, tiled=True)
    key_all = lax.all_to_all(key_rows, "person", split_axis=2, concat_axis=0, tiled=True)
    value_all = lax.all_to_all(value_rows, "person", split_axis=2, concat_axis=0, tiled=True)
    flag_all = lax.all_to_all(spread_flags, "person", split_axis=2, concat_axis=0, tiled=True)
    people = query_all.shape[0]
    scores = jnp.einsum("qfhd,kfhd->fhqk", query_all, key_all, preferred_element_type=jnp.float32)
    persons = jnp.arange(people, dtype=jnp.int32)
    self_pair = persons[:, None] == persons[None, :]
    allowed = (jnp.transpose(flag_all[:, :, 0, 0])[:, None, None, :] > 0) | self_pair[None, None]
    weights = jnp.where(allowed, jnp.exp(scores), 0.0).astype(jnp.bfloat16)
    summed = jnp.einsum("fhqk,kfhd->qfhd", weights, value_all, preferred_element_type=jnp.float32)
    totals = jnp.transpose(jnp.sum(weights.astype(jnp.float32), axis=3), (2, 0, 1))
    results = (summed / totals[..., None]).astype(jnp.bfloat16)
    attended = lax.all_to_all(results, "person", split_axis=0, concat_axis=2, tiled=True)
    branch = jnp.dot(
        attended.reshape(token_count, width), cross_out, preferred_element_type=jnp.float32
    ).reshape(person_rows, frame_rows, width)
    return (stream + branch).astype(jnp.bfloat16)


def solution(mesh):
    placed = (
        P(("groups", "person"), "frame", None),
        P(),
        P(),
        P(),
        P(),
        P(),
        P(),
        P("frame", None),
        P(),
        P(),
        P("frame", None),
        P("groups"),
        P("groups"),
    )
    sizes = dict(mesh.shape)
    fits = sizes == {"groups": 2, "person": 4, "frame": 4}
    return jax.shard_map(
        whole_block if fits else on_device,
        mesh=mesh,
        in_specs=placed,
        out_specs=P(("groups", "person"), "frame", None),
        check_vma=False,
    )
```

```python
import functools
import math

import jax
import jax.numpy as jnp
from jax import lax
from jax.experimental import pallas as pl
from jax.experimental.pallas import tpu as pltpu
from jax.sharding import PartitionSpec as P

H = 16
HD = 64
MESH = pl.DeviceIdType.MESH
F32 = jnp.float32
BF16 = jnp.bfloat16


def block_kernel(
    tokens,
    qkv_time,
    out_time,
    qkv_cross,
    out_cross,
    counts_in,
    present_in,
    norm_time_in,
    norm_cross_in,
    qgain_time_in,
    kgain_time_in,
    qgain_cross_in,
    kgain_cross_in,
    out,
    counts,
    present,
    norm_time,
    norm_cross,
    qgain_time,
    kgain_time,
    qgain_cross,
    kgain_cross,
    tok,
    w_time,
    wo_time,
    w_cross,
    hid,
    att,
    bias,
    mid,
    mid_in,
    res,
    local_sem,
    small_sem,
    tok_send,
    tok_recv,
    z_send,
    z_recv,
    hop_send,
    hop_recv,
    mid_send,
    mid_recv,
    out_send,
    out_recv,
):
    nz, nx = 4, 4
    group = lax.axis_index("groups")
    xc = lax.axis_index("person")
    z = lax.axis_index("frame")
    x, core = xc // 2, xc % 2
    rows, width = hid.shape
    frames = tok.shape[1]
    depth = qkv_cross.shape[0]
    piece = depth // 16
    part = frames // nx

    def zs(d):
        return (z - d + nz) % nz

    def zt(d):
        return (z + d) % nz

    def xs(i):
        return (xc - i + nx) % nx

    def xt(i):
        return (xc + i) % nx

    barrier = pltpu.get_barrier_semaphore()
    for i in range(nx):
        for d in range(nz):
            if i or d:
                pl.semaphore_signal(
                    barrier, inc=1, device_id={"person": xt(i), "frame": zt(d)}, device_id_type=MESH
                )
    pl.semaphore_signal(barrier, inc=1, device_id={"groups": 1 - group}, device_id_type=MESH)
    own = pl.multiple_of(z * depth, depth)
    local = [
        pltpu.make_async_copy(tokens.at[z], tok.at[z], local_sem.at[0]),
        pltpu.make_async_copy(qkv_time, w_time, local_sem.at[1]),
        pltpu.make_async_copy(out_time, wo_time, local_sem.at[2]),
        pltpu.make_async_copy(
            qkv_cross, w_cross.at[pl.ds(own, depth), pl.ds(0, 3 * width)], local_sem.at[3]
        ),
        pltpu.make_async_copy(
            out_cross, w_cross.at[pl.ds(own, depth), pl.ds(3 * width, width)], local_sem.at[4]
        ),
    ]
    small = [
        pltpu.make_async_copy(source, target, small_sem.at[k])
        for k, (source, target) in enumerate(
            (
                (counts_in, counts),
                (present_in, present),
                (norm_time_in, norm_time),
                (norm_cross_in, norm_cross),
                (qgain_time_in, qgain_time),
                (kgain_time_in, kgain_time),
                (qgain_cross_in, qgain_cross),
                (kgain_cross_in, kgain_cross),
            )
        )
    ]
    for copy in small + local:
        copy.start()
    pl.semaphore_wait(barrier, nx * nz)

    def tok_copy(block, slot, d, peer):
        return pltpu.make_async_remote_copy(
            src_ref=tokens.at[block],
            dst_ref=tok.at[slot],
            send_sem=tok_send.at[d - 1],
            recv_sem=tok_recv.at[d - 1],
            device_id={"frame": peer},
            device_id_type=MESH,
        )

    for d in (2, 1, 3):
        tok_copy(zt(d), z, d, zt(d)).start()

    def at_piece(half):
        slot = core * 4 + (group * 2 + x if half == 0 else x * 2 + group)
        return half * (depth // 2) + slot * piece

    def z_copy(half, d, way, shard, peer):
        start = pl.multiple_of(shard * depth + at_piece(half), piece)
        block = w_cross.at[pl.ds(start, piece), :]
        return pltpu.make_async_remote_copy(
            src_ref=block,
            dst_ref=block,
            send_sem=z_send.at[half, d - 1, way],
            recv_sem=z_recv.at[half, d - 1],
            device_id={"frame": peer},
            device_id_type=MESH,
        )

    def pass_on(k, act):
        @pl.when((z + 1 < nz) & (z >= k - 1))
        def _():
            for half in range(2):
                act(z_copy(half, k, 0, zs(k - 1), zt(1)))

        @pl.when((z >= 1) & (z + k - 1 < nz))
        def _():
            for half in range(2):
                act(z_copy(half, nz - k, 1, zt(k - 1), zs(1)))

    def by_arrival(k, act):
        @pl.when(z >= k)
        def _():
            act(k)

        @pl.when(z + k < nz)
        def _():
            act(nz - k)

    local[3].wait()
    local[4].wait()
    pass_on(1, lambda copy: copy.start())

    def hop_copy(hop, half, d, incoming):
        along_x = (half == 0) == (hop == 0)
        if hop == 2:
            side = 1 - core if incoming else core
            offset, length = side * 4, 4
            device = {"person": x * 2 + 1 - core}
        else:
            gx = (1 - x if incoming and along_x else x)
            gy = (1 - group if incoming and not along_x else group)
            if hop == 0:
                offset, length = core * 4 + (gy * 2 + gx if half == 0 else gx * 2 + gy), 1
            else:
                offset, length = core * 4 + (gy if half == 0 else gx) * 2, 2
            device = {"person": (1 - x) * 2 + core} if along_x else {"groups": 1 - group}
        start = pl.multiple_of(
            zs(d) * depth + half * (depth // 2) + offset * piece, length * piece
        )
        block = w_cross.at[pl.ds(start, length * piece), :]
        return pltpu.make_async_remote_copy(
            src_ref=block,
            dst_ref=block,
            send_sem=hop_send.at[hop, half, d - 1],
            recv_sem=hop_recv.at[hop, half, d - 1],
            device_id=device,
            device_id_type=MESH,
        )

    def forward(hop, d):
        for half in range(2):
            if hop == 0:
                z_copy(half, d, 0, zs(d), zs(1)).wait_recv()
            else:
                hop_copy(hop - 1, half, d, True).wait_recv()
        for half in range(2):
            hop_copy(hop, half, d, False).start()

    def arrive(k):
        by_arrival(k, functools.partial(forward, 0))
        if k + 1 < nz:
            pass_on(k + 1, lambda copy: copy.start())

    lane = lax.broadcasted_iota(jnp.int32, (rows, 128), 1)
    low = lane < HD
    same_head = (
        lax.broadcasted_iota(jnp.int32, (256, 256), 0) // HD
        == lax.broadcasted_iota(jnp.int32, (256, 256), 1) // HD
    )
    blocks = jnp.where(same_head, 1.0, 0.0).astype(BF16)
    ones = jnp.ones((rows, 128), BF16)
    key_index = lax.broadcasted_iota(jnp.int32, (rows, rows), 1)
    query_index = lax.broadcasted_iota(jnp.int32, (rows, rows), 0)

    def normed(stream, gains):
        scale = lax.rsqrt(jnp.mean(stream * stream, axis=-1, keepdims=True) + 1e-06)
        return (stream * scale * gains).astype(BF16)

    def attend(weight, qgain, kgain, after):
        hidden = hid[...]
        once = qgain[...] * kgain[...] * (3.0 / math.sqrt(HD))
        gain = jnp.concatenate([once] * 4, axis=1)

        def project(column):
            return jnp.dot(hidden, weight[:, pl.ds(column, 256)], preferred_element_type=F32)

        def unit(entries):
            squares = jnp.dot((entries * entries).astype(BF16), blocks, preferred_element_type=F32)
            return entries * lax.rsqrt(squares * (1.0 / HD) + 1e-06)

        for t in range(width // 256):
            column = t * 256
            queries = unit(project(column)) * gain
            keys = unit(project(width + column)).astype(BF16)
            values = project(2 * width + column).astype(BF16)
            for pair in range(2):
                lanes = slice(pair * 128, (pair + 1) * 128)
                two = queries[:, lanes]
                extended = jnp.concatenate([values[:, lanes], ones], axis=1)
                sums = []
                for member in range(2):
                    one = jnp.where(low if member == 0 else ~low, two, 0.0).astype(BF16)
                    scores = lax.dot_general(
                        one, keys[:, lanes], (((1,), (1,)), ((), ())), preferred_element_type=F32
                    )
                    weights = jnp.exp(scores + bias[...]).astype(BF16)
                    sums.append(jnp.dot(weights, extended, preferred_element_type=F32))
                summed = jnp.where(low, sums[0][:, :128], sums[1][:, :128])
                total = jnp.where(low, sums[0][:, 128:], sums[1][:, 128:])
                att[:, pl.ds(column + pair * 128, 128)] = (summed / total).astype(BF16)
            after(t)

    person = xc * nz + z
    for copy in small:
        copy.wait()
    bias[...] = jnp.where(key_index < counts[person], 0.0, -1e30)
    arrive(1)
    local[0].wait()
    for d in (1, 3, 2):
        tok_copy(zs(d), zs(d), d, zs(d)).wait_recv()
    hid[...] = normed(tok[...].reshape(rows, width).astype(F32), norm_time[...])
    local[1].wait()
    def spread(t):
        if t == 0:
            arrive(2)
        if t == 2:
            arrive(3)
        if t == 3:
            by_arrival(1, functools.partial(forward, 1))

    attend(w_time, qgain_time, kgain_time, spread)
    local[2].wait()

    def temporal_out(t, carry):
        column = pl.multiple_of(t * 256, 256)
        branch = jnp.dot(att[...], wo_time[:, pl.ds(column, 256)], preferred_element_type=F32)
        stream = tok[:, :, pl.ds(column, 256)].reshape(rows, 256).astype(F32)
        mid[:, pl.ds(column, 256)] = (stream + branch).astype(BF16)
        return carry

    lax.fori_loop(0, width // 256, temporal_out, 0)

    def mid_copy(i, d, take_x, take_z, owner, peer):
        start = pl.multiple_of(take_z * frames + take_x * part, part)
        into = pl.multiple_of(owner * part, part)
        return pltpu.make_async_remote_copy(
            src_ref=mid.at[pl.ds(start, part), :],
            dst_ref=mid_in.at[pl.ds(into, part), :],
            send_sem=mid_send.at[i, d],
            recv_sem=mid_recv.at[i, d],
            device_id=peer,
            device_id_type=MESH,
        )

    offsets = [(i, d) for d in (2, 1, 3, 0) for i in range(nx) if i or d]
    for i, d in offsets:
        mid_copy(i, d, xt(i), zt(d), person, {"person": xt(i), "frame": zt(d)}).start()
    into = pl.multiple_of(person * part, part)
    start = pl.multiple_of(z * frames + xc * part, part)
    mid_in[pl.ds(into, part), :] = mid[pl.ds(start, part), :]

    for k in (2, 3):
        by_arrival(k, functools.partial(forward, 1))

    key_row = lax.broadcasted_iota(jnp.int32, (8, rows), 1)
    limit = jnp.zeros((8, rows), jnp.int32)
    for member in range(nx * nz):
        valid = jnp.where(present[member] == 1, counts[member], 0)
        limit = jnp.where(key_row // part == member, valid, limit)
    frame = z * frames + xc * part + key_row % part
    usable = jnp.broadcast_to(jnp.where(frame < limit, 1, 0)[:1, :], (rows, rows))
    allowed = ((key_index % part == query_index % part) & (usable > 0)) | (key_index == query_index)
    bias[...] = jnp.where(allowed, 0.0, -1e30)

    for k in (1, 2, 3):
        by_arrival(k, functools.partial(forward, 2))
    for i, d in offsets:
        source = xs(i) * nz + zs(d)
        mid_copy(i, d, xc, z, source, {"person": xs(i), "frame": zs(d)}).wait_recv()
    hid[...] = normed(mid_in[...].astype(F32), norm_cross[...])
    for d in (1, 3, 2):
        for half in range(2):
            hop_copy(2, half, d, True).wait_recv()
    attend(w_cross, qgain_cross, kgain_cross, lambda t: None)

    def cross_out(t, carry):
        column = pl.multiple_of(t * 256, 256)
        branch = jnp.dot(
            att[...], w_cross[:, pl.ds(3 * width + column, 256)], preferred_element_type=F32
        )
        total = mid_in[:, pl.ds(column, 256)].astype(F32) + branch
        res[:, :, pl.ds(column, 256)] = total.astype(BF16).reshape(nx * nz, part, 256)
        return carry

    lax.fori_loop(0, width // 256, cross_out, 0)

    def out_copy(i, block, slot, peer):
        return pltpu.make_async_remote_copy(
            src_ref=res.at[pl.ds(block * nz, nz)],
            dst_ref=out.at[:, pl.ds(pl.multiple_of(slot * part, part), part), :],
            send_sem=out_send.at[i - 1],
            recv_sem=out_recv.at[i - 1],
            device_id={"person": peer},
            device_id_type=MESH,
        )

    for i in (2, 3, 1):
        out_copy(i, xt(i), xc, xt(i)).start()
    kept = pltpu.make_async_copy(
        res.at[pl.ds(xc * nz, nz)],
        out.at[:, pl.ds(pl.multiple_of(xc * part, part), part), :],
        local_sem.at[5],
    )
    kept.start()
    for d in (1, 2, 3):
        tok_copy(zt(d), z, d, zt(d)).wait_send()
        for half in range(2):
            for hop in range(3):
                hop_copy(hop, half, d, False).wait_send()
        pass_on(d, lambda copy: copy.wait_send())
    for i, d in offsets:
        mid_copy(i, d, xt(i), zt(d), person, {"person": xt(i), "frame": zt(d)}).wait_send()
    kept.wait()
    for i in (1, 2, 3):
        out_copy(i, xt(i), xc, xt(i)).wait_send()
        out_copy(i, xs(i), xs(i), xs(i)).wait_recv()


def whole_block(
    tokens,
    norm_time,
    qkv_time,
    qgain_time,
    kgain_time,
    out_time,
    norm_cross,
    qkv_cross,
    qgain_cross,
    kgain_cross,
    out_cross,
    frame_counts,
    presence,
):
    persons, frames, width = tokens.shape
    rows = persons * frames
    anywhere = pl.BlockSpec(memory_space=pl.ANY)
    dma = pltpu.SemaphoreType.DMA
    return pl.pallas_call(
        block_kernel,
        out_shape=jax.ShapeDtypeStruct(tokens.shape, BF16),
        in_specs=[anywhere] * 13,
        out_specs=anywhere,
        scratch_shapes=[
            pltpu.SMEM(frame_counts.shape, jnp.int32),
            pltpu.SMEM(presence.shape, jnp.int32),
            pltpu.VMEM((1, width), F32),
            pltpu.VMEM((1, width), F32),
            pltpu.VMEM((1, HD), F32),
            pltpu.VMEM((1, HD), F32),
            pltpu.VMEM((1, HD), F32),
            pltpu.VMEM((1, HD), F32),
            pltpu.VMEM(tokens.shape, BF16),
            pltpu.VMEM((width, 3 * width), BF16),
            pltpu.VMEM((width, width), BF16),
            pltpu.VMEM((width, 4 * width), BF16),
            pltpu.VMEM((rows, width), BF16),
            pltpu.VMEM((rows, width), BF16),
            pltpu.VMEM((rows, rows), F32),
            pltpu.VMEM((rows, width), BF16),
            pltpu.VMEM((rows, width), BF16),
            pltpu.VMEM((16, rows // 16, width), BF16),
            dma((6,)),
            dma((8,)),
            dma((3,)),
            dma((3,)),
            dma((2, 3, 2)),
            dma((2, 3)),
            dma((3, 2, 3)),
            dma((3, 2, 3)),
            dma((4, 4)),
            dma((4, 4)),
            dma((3,)),
            dma((3,)),
        ],
        compiler_params=pltpu.CompilerParams(
            collective_id=0, has_side_effects=True, vmem_limit_bytes=60 * 1024 * 1024
        ),
    )(
        tokens,
        qkv_time,
        out_time,
        qkv_cross,
        out_cross,
        frame_counts,
        presence,
        norm_time[None, :],
        norm_cross[None, :],
        qgain_time[None, :],
        kgain_time[None, :],
        qgain_cross[None, :],
        kgain_cross[None, :],
    )


def norm_rows(entries, gains):
    return entries * lax.rsqrt(jnp.mean(entries * entries, axis=-1, keepdims=True) + 1e-06) * gains


def project(hidden, weight, qgain, kgain):
    leading = hidden.shape[:-1]
    flat_rows = hidden.reshape(-1, hidden.shape[-1])
    joined = jnp.dot(flat_rows, weight, preferred_element_type=jnp.float32).reshape(
        leading + (3, H, HD)
    )
    queries = (norm_rows(joined[..., 0, :, :], qgain) * (3.0 / math.sqrt(HD))).astype(jnp.bfloat16)
    key_rows = norm_rows(joined[..., 1, :, :], kgain).astype(jnp.bfloat16)
    value_rows = joined[..., 2, :, :].astype(jnp.bfloat16)
    return (queries, key_rows, value_rows)


def on_device(
    tokens,
    norm_time,
    qkv_time,
    qgain_time,
    kgain_time,
    out_time,
    norm_cross,
    qkv_cross,
    qgain_cross,
    kgain_cross,
    out_cross,
    frame_counts,
    presence,
):
    person_rows, frame_rows, width = tokens.shape
    person_base = lax.axis_index("person") * person_rows
    frame_base = lax.axis_index("frame") * frame_rows
    cross_qkv, cross_out = (
        lax.all_gather(qkv_cross, "frame", axis=0, tiled=True),
        lax.all_gather(out_cross, "frame", axis=0, tiled=True),
    )
    local_counts = lax.dynamic_slice_in_dim(frame_counts, person_base, person_rows)
    local_present = lax.dynamic_slice_in_dim(presence, person_base, person_rows)
    frame_index = frame_base + jnp.arange(frame_rows, dtype=jnp.int32)
    live_frames = frame_index[None, :] < local_counts[:, None]
    key_flags_time = live_frames.astype(jnp.int32)
    key_flags_cross = (live_frames & (local_present[:, None] == 1)).astype(jnp.int32)
    stream = tokens.astype(jnp.float32)
    hidden = norm_rows(stream, norm_time).astype(jnp.bfloat16)
    queries, key_rows, value_rows = project(hidden, qkv_time, qgain_time, kgain_time)
    spread_flags = jnp.broadcast_to(
        key_flags_time[:, :, None, None], (person_rows, frame_rows, H, 1)
    )

    def attend_one(member):
        query_one, key_one, value_one, flag_one = member
        scores = jnp.einsum("qhd,khd->hqk", query_one, key_one, preferred_element_type=jnp.float32)
        allowed = (flag_one[:, 0, 0] > 0)[None, None, :]
        weights = jnp.where(allowed, jnp.exp(scores), 0.0).astype(jnp.bfloat16)
        summed = jnp.einsum("hqk,khd->qhd", weights, value_one, preferred_element_type=jnp.float32)
        totals = jnp.transpose(jnp.sum(weights.astype(jnp.float32), axis=-1))
        return (summed / totals[:, :, None]).astype(jnp.bfloat16)

    results = lax.map(
        attend_one,
        (
            lax.all_to_all(queries, "frame", split_axis=2, concat_axis=1, tiled=True),
            lax.all_to_all(key_rows, "frame", split_axis=2, concat_axis=1, tiled=True),
            lax.all_to_all(value_rows, "frame", split_axis=2, concat_axis=1, tiled=True),
            lax.all_to_all(spread_flags, "frame", split_axis=2, concat_axis=1, tiled=True),
        ),
    )
    attended = lax.all_to_all(results, "frame", split_axis=1, concat_axis=2, tiled=True)
    token_count = person_rows * frame_rows
    branch = jnp.dot(
        attended.reshape(token_count, width), out_time, preferred_element_type=jnp.float32
    ).reshape(person_rows, frame_rows, width)
    middle = (stream + branch).astype(jnp.bfloat16)
    middle = lax.optimization_barrier(middle)
    stream = middle.astype(jnp.float32)
    hidden = norm_rows(stream, norm_cross).astype(jnp.bfloat16)
    queries, key_rows, value_rows = project(hidden, cross_qkv, qgain_cross, kgain_cross)
    spread_flags = jnp.broadcast_to(
        key_flags_cross[:, :, None, None], (person_rows, frame_rows, H, 1)
    )
    query_all = lax.all_to_all(queries, "person", split_axis=2, concat_axis=0, tiled=True)
    key_all = lax.all_to_all(key_rows, "person", split_axis=2, concat_axis=0, tiled=True)
    value_all = lax.all_to_all(value_rows, "person", split_axis=2, concat_axis=0, tiled=True)
    flag_all = lax.all_to_all(spread_flags, "person", split_axis=2, concat_axis=0, tiled=True)
    people = query_all.shape[0]
    scores = jnp.einsum("qfhd,kfhd->fhqk", query_all, key_all, preferred_element_type=jnp.float32)
    persons = jnp.arange(people, dtype=jnp.int32)
    self_pair = persons[:, None] == persons[None, :]
    allowed = (jnp.transpose(flag_all[:, :, 0, 0])[:, None, None, :] > 0) | self_pair[None, None]
    weights = jnp.where(allowed, jnp.exp(scores), 0.0).astype(jnp.bfloat16)
    summed = jnp.einsum("fhqk,kfhd->qfhd", weights, value_all, preferred_element_type=jnp.float32)
    totals = jnp.transpose(jnp.sum(weights.astype(jnp.float32), axis=3), (2, 0, 1))
    results = (summed / totals[..., None]).astype(jnp.bfloat16)
    attended = lax.all_to_all(results, "person", split_axis=0, concat_axis=2, tiled=True)
    branch = jnp.dot(
        attended.reshape(token_count, width), cross_out, preferred_element_type=jnp.float32
    ).reshape(person_rows, frame_rows, width)
    return (stream + branch).astype(jnp.bfloat16)


def solution(mesh):
    placed = (
        P(("groups", "person"), "frame", None),
        P(),
        P(),
        P(),
        P(),
        P(),
        P(),
        P("frame", None),
        P(),
        P(),
        P("frame", None),
        P("groups"),
        P("groups"),
    )
    sizes = dict(mesh.shape)
    fits = sizes == {"groups": 2, "person": 4, "frame": 4}
    return jax.shard_map(
        whole_block if fits else on_device,
        mesh=mesh,
        in_specs=placed,
        out_specs=P(("groups", "person"), "frame", None),
        check_vma=False,
    )
```

```python
import functools
import math

import jax
import jax.numpy as jnp
from jax import lax
from jax.experimental import pallas as pl
from jax.experimental.pallas import tpu as pltpu
from jax.sharding import PartitionSpec as P

H = 16
HD = 64
MESH = pl.DeviceIdType.MESH
F32 = jnp.float32
BF16 = jnp.bfloat16


def block_kernel(
    tokens,
    qkv_time,
    out_time,
    qkv_cross,
    out_cross,
    counts_in,
    present_in,
    norm_time_in,
    norm_cross_in,
    qgain_time_in,
    kgain_time_in,
    qgain_cross_in,
    kgain_cross_in,
    out,
    counts,
    present,
    norm_time,
    norm_cross,
    qgain_time,
    kgain_time,
    qgain_cross,
    kgain_cross,
    tok,
    w_time,
    wo_time,
    w_cross,
    hid,
    att,
    bias,
    mid,
    mid_in,
    res,
    local_sem,
    small_sem,
    tok_send,
    tok_recv,
    z_send,
    z_recv,
    hop_send,
    hop_recv,
    mid_send,
    mid_recv,
    out_send,
    out_recv,
):
    nz, nx = 4, 4
    group = lax.axis_index("groups")
    xc = lax.axis_index("person")
    z = lax.axis_index("frame")
    x, core = xc // 2, xc % 2
    rows, width = hid.shape
    frames = tok.shape[1]
    depth = qkv_cross.shape[0]
    piece = depth // 16
    part = frames // nx

    def zs(d):
        return (z - d + nz) % nz

    def zt(d):
        return (z + d) % nz

    def xs(i):
        return (xc - i + nx) % nx

    def xt(i):
        return (xc + i) % nx

    barrier = pltpu.get_barrier_semaphore()
    for i in range(nx):
        for d in range(nz):
            if i or d:
                pl.semaphore_signal(
                    barrier, inc=1, device_id={"person": xt(i), "frame": zt(d)}, device_id_type=MESH
                )
    pl.semaphore_signal(barrier, inc=1, device_id={"groups": 1 - group}, device_id_type=MESH)
    own = pl.multiple_of(z * depth, depth)
    local = [
        pltpu.make_async_copy(tokens.at[z], tok.at[z], local_sem.at[0]),
        pltpu.make_async_copy(qkv_time, w_time, local_sem.at[1]),
        pltpu.make_async_copy(out_time, wo_time, local_sem.at[2]),
        pltpu.make_async_copy(
            qkv_cross, w_cross.at[pl.ds(own, depth), pl.ds(0, 3 * width)], local_sem.at[3]
        ),
        pltpu.make_async_copy(
            out_cross, w_cross.at[pl.ds(own, depth), pl.ds(3 * width, width)], local_sem.at[4]
        ),
    ]
    small = [
        pltpu.make_async_copy(source, target, small_sem.at[k])
        for k, (source, target) in enumerate(
            (
                (counts_in, counts),
                (present_in, present),
                (norm_time_in, norm_time),
                (norm_cross_in, norm_cross),
                (qgain_time_in, qgain_time),
                (kgain_time_in, kgain_time),
                (qgain_cross_in, qgain_cross),
                (kgain_cross_in, kgain_cross),
            )
        )
    ]
    for copy in local[3:] + local[:3] + small:
        copy.start()
    pl.semaphore_wait(barrier, nx * nz)

    def tok_copy(block, slot, d, peer):
        return pltpu.make_async_remote_copy(
            src_ref=tokens.at[block],
            dst_ref=tok.at[slot],
            send_sem=tok_send.at[d - 1],
            recv_sem=tok_recv.at[d - 1],
            device_id={"frame": peer},
            device_id_type=MESH,
        )

    def at_piece(half):
        slot = core * 4 + (group * 2 + x if half == 0 else x * 2 + group)
        return half * (depth // 2) + slot * piece

    def z_copy(half, d, way, shard, peer):
        start = pl.multiple_of(shard * depth + at_piece(half), piece)
        block = w_cross.at[pl.ds(start, piece), :]
        return pltpu.make_async_remote_copy(
            src_ref=block,
            dst_ref=block,
            send_sem=z_send.at[half, d - 1, way],
            recv_sem=z_recv.at[half, d - 1],
            device_id={"frame": peer},
            device_id_type=MESH,
        )

    def pass_on(k, act):
        @pl.when((z + 1 < nz) & (z >= k - 1))
        def _():
            for half in range(2):
                act(z_copy(half, k, 0, zs(k - 1), zt(1)))

        @pl.when((z >= 1) & (z + k - 1 < nz))
        def _():
            for half in range(2):
                act(z_copy(half, nz - k, 1, zt(k - 1), zs(1)))

    def by_arrival(k, act):
        @pl.when(z >= k)
        def _():
            act(k)

        @pl.when(z + k < nz)
        def _():
            act(nz - k)

    local[3].wait()
    local[4].wait()
    pass_on(1, lambda copy: copy.start())
    for d in (2, 1, 3):
        tok_copy(zt(d), z, d, zt(d)).start()

    def hop_copy(hop, half, d, incoming, columns=None):
        along_x = (half == 0) == (hop == 0)
        if hop == 2:
            side = 1 - core if incoming else core
            offset, length = side * 4, 4
            device = {"person": x * 2 + 1 - core}
        else:
            gx = (1 - x if incoming and along_x else x)
            gy = (1 - group if incoming and not along_x else group)
            if hop == 0:
                offset, length = core * 4 + (gy * 2 + gx if half == 0 else gx * 2 + gy), 1
            else:
                offset, length = core * 4 + (gy if half == 0 else gx) * 2, 2
            device = {"person": (1 - x) * 2 + core} if along_x else {"groups": 1 - group}
        start = pl.multiple_of(
            zs(d) * depth + half * (depth // 2) + offset * piece, length * piece
        )
        first, count = ((0, 4), (0, 3), (3, 1))[0 if columns is None else columns + 1]
        block = w_cross.at[pl.ds(start, length * piece), pl.ds(first * width, count * width)]
        slot = hop if columns is None else hop + columns
        return pltpu.make_async_remote_copy(
            src_ref=block,
            dst_ref=block,
            send_sem=hop_send.at[slot, half, d - 1],
            recv_sem=hop_recv.at[slot, half, d - 1],
            device_id=device,
            device_id_type=MESH,
        )

    def forward(hop, d):
        for half in range(2):
            if hop == 0:
                z_copy(half, d, 0, zs(d), zs(1)).wait_recv()
            else:
                hop_copy(hop - 1, half, d, True).wait_recv()
        for half in range(2):
            hop_copy(hop, half, d, False, 0 if hop == 2 else None).start()

    def arrive(k):
        by_arrival(k, functools.partial(forward, 0))
        if k + 1 < nz:
            pass_on(k + 1, lambda copy: copy.start())

    lane = lax.broadcasted_iota(jnp.int32, (rows, 128), 1)
    low = lane < HD
    same_head = (
        lax.broadcasted_iota(jnp.int32, (256, 256), 0) // HD
        == lax.broadcasted_iota(jnp.int32, (256, 256), 1) // HD
    )
    blocks = jnp.where(same_head, 1.0, 0.0).astype(BF16)
    ones = jnp.ones((rows, 128), BF16)
    key_index = lax.broadcasted_iota(jnp.int32, (rows, rows), 1)
    query_index = lax.broadcasted_iota(jnp.int32, (rows, rows), 0)

    def normed(stream, gains):
        scale = lax.rsqrt(jnp.mean(stream * stream, axis=-1, keepdims=True) + 1e-06)
        return (stream * scale * gains).astype(BF16)

    def attend(weight, qgain, kgain, after):
        hidden = hid[...]
        once = qgain[...] * kgain[...] * (3.0 / math.sqrt(HD))
        gain = jnp.concatenate([once] * 4, axis=1)

        def project(column):
            return jnp.dot(hidden, weight[:, pl.ds(column, 256)], preferred_element_type=F32)

        def unit(entries):
            squares = jnp.dot((entries * entries).astype(BF16), blocks, preferred_element_type=F32)
            return entries * lax.rsqrt(squares * (1.0 / HD) + 1e-06)

        for t in range(width // 256):
            column = t * 256
            queries = unit(project(column)) * gain
            keys = unit(project(width + column)).astype(BF16)
            values = project(2 * width + column).astype(BF16)
            for pair in range(2):
                lanes = slice(pair * 128, (pair + 1) * 128)
                two = queries[:, lanes]
                extended = jnp.concatenate([values[:, lanes], ones], axis=1)
                sums = []
                for member in range(2):
                    one = jnp.where(low if member == 0 else ~low, two, 0.0).astype(BF16)
                    scores = lax.dot_general(
                        one, keys[:, lanes], (((1,), (1,)), ((), ())), preferred_element_type=F32
                    )
                    weights = jnp.exp(scores + bias[...]).astype(BF16)
                    sums.append(jnp.dot(weights, extended, preferred_element_type=F32))
                summed = jnp.where(low, sums[0][:, :128], sums[1][:, :128])
                total = jnp.where(low, sums[0][:, 128:], sums[1][:, 128:])
                att[:, pl.ds(column + pair * 128, 128)] = (summed / total).astype(BF16)
            after(t)

    person = xc * nz + z
    for copy in small:
        copy.wait()
    bias[...] = jnp.where(key_index < counts[person], 0.0, -1e30)
    arrive(1)
    local[0].wait()
    for d in (1, 3, 2):
        tok_copy(zs(d), zs(d), d, zs(d)).wait_recv()
    hid[...] = normed(tok[...].reshape(rows, width).astype(F32), norm_time[...])
    arrive(2)
    local[1].wait()
    def spread(t):
        if t == 1:
            by_arrival(1, functools.partial(forward, 1))
            arrive(3)
        if t == 3:
            by_arrival(2, functools.partial(forward, 1))

    attend(w_time, qgain_time, kgain_time, spread)
    local[2].wait()

    def temporal_out(t, carry):
        column = pl.multiple_of(t * 256, 256)
        branch = jnp.dot(att[...], wo_time[:, pl.ds(column, 256)], preferred_element_type=F32)
        stream = tok[:, :, pl.ds(column, 256)].reshape(rows, 256).astype(F32)
        mid[:, pl.ds(column, 256)] = (stream + branch).astype(BF16)
        return carry

    lax.fori_loop(0, width // 256, temporal_out, 0)

    def mid_copy(i, d, take_x, take_z, owner, peer):
        start = pl.multiple_of(take_z * frames + take_x * part, part)
        into = pl.multiple_of(owner * part, part)
        return pltpu.make_async_remote_copy(
            src_ref=mid.at[pl.ds(start, part), :],
            dst_ref=mid_in.at[pl.ds(into, part), :],
            send_sem=mid_send.at[i, d],
            recv_sem=mid_recv.at[i, d],
            device_id=peer,
            device_id_type=MESH,
        )

    offsets = [(i, d) for d in (2, 1, 3, 0) for i in range(nx) if i or d]
    for i, d in offsets:
        mid_copy(i, d, xt(i), zt(d), person, {"person": xt(i), "frame": zt(d)}).start()
    into = pl.multiple_of(person * part, part)
    start = pl.multiple_of(z * frames + xc * part, part)
    mid_in[pl.ds(into, part), :] = mid[pl.ds(start, part), :]

    by_arrival(3, functools.partial(forward, 1))

    key_row = lax.broadcasted_iota(jnp.int32, (8, rows), 1)
    limit = jnp.zeros((8, rows), jnp.int32)
    for member in range(nx * nz):
        valid = jnp.where(present[member] == 1, counts[member], 0)
        limit = jnp.where(key_row // part == member, valid, limit)
    frame = z * frames + xc * part + key_row % part
    usable = jnp.broadcast_to(jnp.where(frame < limit, 1, 0)[:1, :], (rows, rows))
    allowed = ((key_index % part == query_index % part) & (usable > 0)) | (key_index == query_index)
    bias[...] = jnp.where(allowed, 0.0, -1e30)

    for k in (1, 2, 3):
        by_arrival(k, functools.partial(forward, 2))
    for d in (1, 2, 3):
        for half in range(2):
            hop_copy(2, half, d, False, 1).start()
    for i, d in offsets:
        source = xs(i) * nz + zs(d)
        mid_copy(i, d, xc, z, source, {"person": xs(i), "frame": zs(d)}).wait_recv()
    hid[...] = normed(mid_in[...].astype(F32), norm_cross[...])
    for d in (1, 3, 2):
        for half in range(2):
            hop_copy(2, half, d, True, 0).wait_recv()
    attend(w_cross, qgain_cross, kgain_cross, lambda t: None)

    for d in (1, 2, 3):
        for half in range(2):
            hop_copy(2, half, d, True, 1).wait_recv()

    def cross_out(t, carry):
        column = pl.multiple_of(t * 256, 256)
        branch = jnp.dot(
            att[...], w_cross[:, pl.ds(3 * width + column, 256)], preferred_element_type=F32
        )
        total = mid_in[:, pl.ds(column, 256)].astype(F32) + branch
        res[:, :, pl.ds(column, 256)] = total.astype(BF16).reshape(nx * nz, part, 256)
        return carry

    lax.fori_loop(0, width // 256, cross_out, 0)

    def out_copy(i, block, slot, peer):
        return pltpu.make_async_remote_copy(
            src_ref=res.at[pl.ds(block * nz, nz)],
            dst_ref=out.at[:, pl.ds(pl.multiple_of(slot * part, part), part), :],
            send_sem=out_send.at[i - 1],
            recv_sem=out_recv.at[i - 1],
            device_id={"person": peer},
            device_id_type=MESH,
        )

    for i in (2, 3, 1):
        out_copy(i, xt(i), xc, xt(i)).start()
    kept = pltpu.make_async_copy(
        res.at[pl.ds(xc * nz, nz)],
        out.at[:, pl.ds(pl.multiple_of(xc * part, part), part), :],
        local_sem.at[5],
    )
    kept.start()
    for d in (1, 2, 3):
        tok_copy(zt(d), z, d, zt(d)).wait_send()
        for half in range(2):
            for hop in range(2):
                hop_copy(hop, half, d, False).wait_send()
            for columns in range(2):
                hop_copy(2, half, d, False, columns).wait_send()
        pass_on(d, lambda copy: copy.wait_send())
    for i, d in offsets:
        mid_copy(i, d, xt(i), zt(d), person, {"person": xt(i), "frame": zt(d)}).wait_send()
    kept.wait()
    for i in (1, 2, 3):
        out_copy(i, xt(i), xc, xt(i)).wait_send()
        out_copy(i, xs(i), xs(i), xs(i)).wait_recv()


def whole_block(
    tokens,
    norm_time,
    qkv_time,
    qgain_time,
    kgain_time,
    out_time,
    norm_cross,
    qkv_cross,
    qgain_cross,
    kgain_cross,
    out_cross,
    frame_counts,
    presence,
):
    persons, frames, width = tokens.shape
    rows = persons * frames
    anywhere = pl.BlockSpec(memory_space=pl.ANY)
    dma = pltpu.SemaphoreType.DMA
    return pl.pallas_call(
        block_kernel,
        out_shape=jax.ShapeDtypeStruct(tokens.shape, BF16),
        in_specs=[anywhere] * 13,
        out_specs=anywhere,
        scratch_shapes=[
            pltpu.SMEM(frame_counts.shape, jnp.int32),
            pltpu.SMEM(presence.shape, jnp.int32),
            pltpu.VMEM((1, width), F32),
            pltpu.VMEM((1, width), F32),
            pltpu.VMEM((1, HD), F32),
            pltpu.VMEM((1, HD), F32),
            pltpu.VMEM((1, HD), F32),
            pltpu.VMEM((1, HD), F32),
            pltpu.VMEM(tokens.shape, BF16),
            pltpu.VMEM((width, 3 * width), BF16),
            pltpu.VMEM((width, width), BF16),
            pltpu.VMEM((width, 4 * width), BF16),
            pltpu.VMEM((rows, width), BF16),
            pltpu.VMEM((rows, width), BF16),
            pltpu.VMEM((rows, rows), F32),
            pltpu.VMEM((rows, width), BF16),
            pltpu.VMEM((rows, width), BF16),
            pltpu.VMEM((16, rows // 16, width), BF16),
            dma((6,)),
            dma((8,)),
            dma((3,)),
            dma((3,)),
            dma((2, 3, 2)),
            dma((2, 3)),
            dma((4, 2, 3)),
            dma((4, 2, 3)),
            dma((4, 4)),
            dma((4, 4)),
            dma((3,)),
            dma((3,)),
        ],
        compiler_params=pltpu.CompilerParams(
            collective_id=0, has_side_effects=True, vmem_limit_bytes=60 * 1024 * 1024
        ),
    )(
        tokens,
        qkv_time,
        out_time,
        qkv_cross,
        out_cross,
        frame_counts,
        presence,
        norm_time[None, :],
        norm_cross[None, :],
        qgain_time[None, :],
        kgain_time[None, :],
        qgain_cross[None, :],
        kgain_cross[None, :],
    )


def norm_rows(entries, gains):
    return entries * lax.rsqrt(jnp.mean(entries * entries, axis=-1, keepdims=True) + 1e-06) * gains


def project(hidden, weight, qgain, kgain):
    leading = hidden.shape[:-1]
    flat_rows = hidden.reshape(-1, hidden.shape[-1])
    joined = jnp.dot(flat_rows, weight, preferred_element_type=jnp.float32).reshape(
        leading + (3, H, HD)
    )
    queries = (norm_rows(joined[..., 0, :, :], qgain) * (3.0 / math.sqrt(HD))).astype(jnp.bfloat16)
    key_rows = norm_rows(joined[..., 1, :, :], kgain).astype(jnp.bfloat16)
    value_rows = joined[..., 2, :, :].astype(jnp.bfloat16)
    return (queries, key_rows, value_rows)


def on_device(
    tokens,
    norm_time,
    qkv_time,
    qgain_time,
    kgain_time,
    out_time,
    norm_cross,
    qkv_cross,
    qgain_cross,
    kgain_cross,
    out_cross,
    frame_counts,
    presence,
):
    person_rows, frame_rows, width = tokens.shape
    person_base = lax.axis_index("person") * person_rows
    frame_base = lax.axis_index("frame") * frame_rows
    cross_qkv, cross_out = (
        lax.all_gather(qkv_cross, "frame", axis=0, tiled=True),
        lax.all_gather(out_cross, "frame", axis=0, tiled=True),
    )
    local_counts = lax.dynamic_slice_in_dim(frame_counts, person_base, person_rows)
    local_present = lax.dynamic_slice_in_dim(presence, person_base, person_rows)
    frame_index = frame_base + jnp.arange(frame_rows, dtype=jnp.int32)
    live_frames = frame_index[None, :] < local_counts[:, None]
    key_flags_time = live_frames.astype(jnp.int32)
    key_flags_cross = (live_frames & (local_present[:, None] == 1)).astype(jnp.int32)
    stream = tokens.astype(jnp.float32)
    hidden = norm_rows(stream, norm_time).astype(jnp.bfloat16)
    queries, key_rows, value_rows = project(hidden, qkv_time, qgain_time, kgain_time)
    spread_flags = jnp.broadcast_to(
        key_flags_time[:, :, None, None], (person_rows, frame_rows, H, 1)
    )

    def attend_one(member):
        query_one, key_one, value_one, flag_one = member
        scores = jnp.einsum("qhd,khd->hqk", query_one, key_one, preferred_element_type=jnp.float32)
        allowed = (flag_one[:, 0, 0] > 0)[None, None, :]
        weights = jnp.where(allowed, jnp.exp(scores), 0.0).astype(jnp.bfloat16)
        summed = jnp.einsum("hqk,khd->qhd", weights, value_one, preferred_element_type=jnp.float32)
        totals = jnp.transpose(jnp.sum(weights.astype(jnp.float32), axis=-1))
        return (summed / totals[:, :, None]).astype(jnp.bfloat16)

    results = lax.map(
        attend_one,
        (
            lax.all_to_all(queries, "frame", split_axis=2, concat_axis=1, tiled=True),
            lax.all_to_all(key_rows, "frame", split_axis=2, concat_axis=1, tiled=True),
            lax.all_to_all(value_rows, "frame", split_axis=2, concat_axis=1, tiled=True),
            lax.all_to_all(spread_flags, "frame", split_axis=2, concat_axis=1, tiled=True),
        ),
    )
    attended = lax.all_to_all(results, "frame", split_axis=1, concat_axis=2, tiled=True)
    token_count = person_rows * frame_rows
    branch = jnp.dot(
        attended.reshape(token_count, width), out_time, preferred_element_type=jnp.float32
    ).reshape(person_rows, frame_rows, width)
    middle = (stream + branch).astype(jnp.bfloat16)
    middle = lax.optimization_barrier(middle)
    stream = middle.astype(jnp.float32)
    hidden = norm_rows(stream, norm_cross).astype(jnp.bfloat16)
    queries, key_rows, value_rows = project(hidden, cross_qkv, qgain_cross, kgain_cross)
    spread_flags = jnp.broadcast_to(
        key_flags_cross[:, :, None, None], (person_rows, frame_rows, H, 1)
    )
    query_all = lax.all_to_all(queries, "person", split_axis=2, concat_axis=0, tiled=True)
    key_all = lax.all_to_all(key_rows, "person", split_axis=2, concat_axis=0, tiled=True)
    value_all = lax.all_to_all(value_rows, "person", split_axis=2, concat_axis=0, tiled=True)
    flag_all = lax.all_to_all(spread_flags, "person", split_axis=2, concat_axis=0, tiled=True)
    people = query_all.shape[0]
    scores = jnp.einsum("qfhd,kfhd->fhqk", query_all, key_all, preferred_element_type=jnp.float32)
    persons = jnp.arange(people, dtype=jnp.int32)
    self_pair = persons[:, None] == persons[None, :]
    allowed = (jnp.transpose(flag_all[:, :, 0, 0])[:, None, None, :] > 0) | self_pair[None, None]
    weights = jnp.where(allowed, jnp.exp(scores), 0.0).astype(jnp.bfloat16)
    summed = jnp.einsum("fhqk,kfhd->qfhd", weights, value_all, preferred_element_type=jnp.float32)
    totals = jnp.transpose(jnp.sum(weights.astype(jnp.float32), axis=3), (2, 0, 1))
    results = (summed / totals[..., None]).astype(jnp.bfloat16)
    attended = lax.all_to_all(results, "person", split_axis=0, concat_axis=2, tiled=True)
    branch = jnp.dot(
        attended.reshape(token_count, width), cross_out, preferred_element_type=jnp.float32
    ).reshape(person_rows, frame_rows, width)
    return (stream + branch).astype(jnp.bfloat16)


def solution(mesh):
    placed = (
        P(("groups", "person"), "frame", None),
        P(),
        P(),
        P(),
        P(),
        P(),
        P(),
        P("frame", None),
        P(),
        P(),
        P("frame", None),
        P("groups"),
        P("groups"),
    )
    sizes = dict(mesh.shape)
    fits = sizes == {"groups": 2, "person": 4, "frame": 4}
    return jax.shard_map(
        whole_block if fits else on_device,
        mesh=mesh,
        in_specs=placed,
        out_specs=P(("groups", "person"), "frame", None),
        check_vma=False,
    )
```
